32 devices in a mesh: dp: 8 (over y, x, core), pencil: 4 (over z).
Axes of the slice: x: 2, y: 2, z: 4, core: 2. Of those that a mesh axis runs over, the one named last changes fastest.
Arguments:
- jacobian: bfloat16 [8, 8, 24, 1024], P(None, 'pencil', None, 'dp'), may hold values from -0.15625 to 0.15625
- band_offsets: int32 [3, 3], replicated, may hold values from 1 to 4
- band_masks: int32 [3, 3, 4], replicated, may hold values 0 or 1
- band_weights: float32 [3, 3], replicated, may hold values from 0.2 to 0.6
Outputs:
- gram: float32 [1024, 1024], P('dp', 'pencil')
The draws below stay inside these ranges and needn't reach their ends.
All inputs are finite; a program needn't handle non-finite values.
Results may differ from the reference program's by a relative error of at most 0.0047.
Values may be sent and summed in bfloat16 or wider, within the bound.
No kernel may reach another device: no remote copies, remote signals or barrier semaphores. Data moves between devices by JAX's collectives and lax.ppermute only.
A program may use at most 64 MiB of HBM per device.

```python
import math
import jax
import jax.numpy as jnp
from jax import lax

NZ = 24
BANDS = 3
BLOCKS = 4
NX = 8
NY = 8
M = 1024


def with_ends(array, key, least, top_value):
    index_at = [jax.random.randint(jax.random.fold_in(key, axis), (), 0, length) for axis, length in enumerate(array.shape)]
    widest = array.shape.index(max(array.shape))
    next_to = index_at[:widest] + [(index_at[widest] + 1) % array.shape[widest]] + index_at[widest + 1:]
    return array.at[tuple(index_at)].set(least).at[tuple(next_to)].set(top_value)


def level_of(rng, dims, shards, least, largest):
    loudness, own = 1.0, jax.random.fold_in(rng, 6)
    for dim, blocks in shards:
        steps = jnp.exp(jax.random.uniform(jax.random.fold_in(own, dim), (blocks,), jnp.float32, least / len(shards), largest / len(shards)))
        loudness = loudness * jnp.repeat(steps, dims[dim] // blocks).reshape([-1 if axis == dim else 1 for axis in range(len(dims))])
    return loudness


def gaussian(rng, dims, scale, most, shards=(), kind=jnp.bfloat16):
    values = jax.random.normal(rng, dims, jnp.float32) * scale
    if len(shards) > 0:
        values = level_of(rng, dims, shards, -0.22, 0.18) * values
    return jnp.clip(values, min=-most, max=most).astype(kind)


def setup_inputs(seed: int = 0) -> dict:
    arg_keys = jax.random.split(jax.random.key(seed), 5)
    jacobian = gaussian(arg_keys[0], (NX, NY, NZ, M), (NX * NY * NZ) ** -0.5, 0.15625, ((1, 4), (3, 8)))
    band_offsets = with_ends(jax.random.randint(arg_keys[1], (3, BANDS), 1, min(min(NX, NY), NZ) // 2 + 1), jax.random.fold_in(arg_keys[1], 1), 1, (min(min(NX, NY), NZ) // 2 + 1) - 1).astype(jnp.int32)
    band_masks = with_ends((jax.random.randint(arg_keys[2], (3, BANDS, BLOCKS), 0, 2) < 1).astype(jnp.int32), jax.random.fold_in(arg_keys[2], 1), 0, 1)
    band_weights = jnp.clip(jnp.exp(jax.random.uniform(arg_keys[3], (3, BANDS), jnp.float32, math.log(0.2), math.log(0.6))), 0.2, 0.6)
    return dict(jacobian=jacobian, band_offsets=band_offsets, band_masks=band_masks, band_weights=band_weights)


def smoother(length, offsets_row, masks_row, weights_row):
    row_index = lax.broadcasted_iota(jnp.int32, (length, length), 0)
    col_index = lax.broadcasted_iota(jnp.int32, (length, length), 1)
    block_of_row = row_index // (length // BLOCKS)
    matrix = jnp.where(row_index == col_index, jnp.float32(1.0), jnp.float32(0.0))
    for which_band in range(BANDS):
        active = jnp.zeros((length, length), jnp.float32)
        for which_block in range(BLOCKS):
            active = active + jnp.where(block_of_row == which_block, masks_row[which_band, which_block].astype(jnp.float32), jnp.float32(0.0))
        band_reach = offsets_row[which_band]
        placed = (col_index == row_index + band_reach) | (col_index == row_index - band_reach)
        matrix = matrix + jnp.where(placed, active * weights_row[which_band], jnp.float32(0.0))
    return matrix.astype(jnp.bfloat16)


def widen(values):
    return lax.optimization_barrier(values).astype(jnp.float32)


def reference(jacobian, band_offsets, band_masks, band_weights):
    smooth_x = widen(smoother(NX, band_offsets[0], band_masks[0], band_weights[0]))
    smooth_y = widen(smoother(NY, band_offsets[1], band_masks[1], band_weights[1]))
    smooth_z = widen(smoother(NZ, band_offsets[2], band_masks[2], band_weights[2]))
    highest = lax.Precision.HIGHEST
    along_x = jnp.einsum("ax,xyzr->ayzr", smooth_x, jacobian.astype(jnp.float32), precision=highest).astype(jnp.bfloat16)
    along_y = jnp.einsum("by,xyzr->xbzr", smooth_y, widen(along_x), precision=highest).astype(jnp.bfloat16)
    panel = jnp.einsum("cz,xyzr->xycr", smooth_z, widen(along_y), precision=highest).astype(jnp.bfloat16)
    flattened = widen(panel).reshape(-1, M)
    return jnp.dot(flattened.T, flattened, precision=highest)
```

```python
import functools

import jax
import jax.numpy as jnp
from jax import lax
from jax.experimental import pallas as pl
from jax.experimental.pallas import tpu as pltpu
from jax.sharding import PartitionSpec as P

BANDS = 3
BLOCKS = 4
LANES = 128
CORES = 2
COLUMNS_AT_ONCE = 8
VMEM = pl.BlockSpec(memory_space=pltpu.VMEM)
SMEM = pl.BlockSpec(memory_space=pltpu.SMEM)


def farthest(rank, plane, planes):
    mirrored = planes - 1 - plane
    if isinstance(plane, int) and isinstance(rank, int):
        alone, reach, outer = abs(plane - mirrored), min(plane, mirrored), rank if plane > mirrored else planes - 1 - rank
        pair = rank - alone
        inner = plane - (reach - pair // 2) if pair % 2 == 0 else plane + (reach - pair // 2)
        return outer if rank < alone else inner
    alone, reach = jnp.abs(plane - mirrored), jnp.minimum(plane, mirrored)
    outer = jnp.where(plane > mirrored, rank, planes - 1 - rank)
    pair = rank - alone
    away = reach - (pair >> 1)
    inner = jnp.where((pair & 1) == 0, plane - away, plane + away)
    return jnp.where(rank < alone, outer, inner)


def smoother(distance, owner, axis, length, offsets, masks, weights):
    matrix = jnp.where(distance == 0, jnp.float32(1.0), jnp.float32(0.0))
    for band in range(BANDS):
        value = masks[axis, band, 0].astype(jnp.float32) * weights[axis, band]
        for block in range(1, BLOCKS):
            here = masks[axis, band, block].astype(jnp.float32) * weights[axis, band]
            value = jnp.where(owner >= block * (length // BLOCKS), here, value)
        matrix = matrix + jnp.where(distance == offsets[axis, band], value, jnp.float32(0.0))
    return matrix.astype(jnp.bfloat16)


def write_gram(table, axis, length, params):
    row = lax.broadcasted_iota(jnp.int32, (LANES, LANES), 0)
    col = lax.broadcasted_iota(jnp.int32, (LANES, LANES), 1)
    distance = jnp.where((row < length) & (col < length), jnp.abs(row - col), -1)
    gram = jnp.dot(
        smoother(distance, col, axis, length, *params),
        smoother(distance, row, axis, length, *params),
        preferred_element_type=jnp.float32,
    )
    for place in range(length):
        table[place] = jnp.broadcast_to(gram[:length, place : place + 1], (length, LANES))


def mix_x_z_kernel(dims, offsets, masks, weights, field, out, along_z, table):
    length_x, width, depth = dims
    params = (offsets, masks, weights)
    write_gram(table, 0, length_x, params)
    rows = COLUMNS_AT_ONCE * depth
    shape = (COLUMNS_AT_ONCE, depth, rows)
    row_z = lax.broadcasted_iota(jnp.int32, shape, 1)
    row_group = lax.broadcasted_iota(jnp.int32, shape, 0)
    lane = lax.broadcasted_iota(jnp.int32, shape, 2)
    lane_group = jnp.zeros(shape, jnp.int32)
    for group in range(1, COLUMNS_AT_ONCE):
        lane_group = lane_group + jnp.where(lane >= group * depth, 1, 0)
    lane_z = lane - lane_group * depth
    distance = jnp.where(row_group == lane_group, jnp.abs(row_z - lane_z), -1)
    forth = smoother(distance, row_z, 2, depth, *params).astype(jnp.float32).reshape(rows, rows).astype(jnp.bfloat16)
    back = smoother(distance, lane_z, 2, depth, *params).astype(jnp.float32).reshape(rows, rows).astype(jnp.bfloat16)
    pieces = length_x * width // COLUMNS_AT_ONCE
    for first in range(0, pieces, 2):
        held = jnp.concatenate([field[piece * rows : (piece + 1) * rows, :] for piece in (first, first + 1)], axis=1)
        once = jnp.dot(forth, held, preferred_element_type=jnp.float32)
        high = once.astype(jnp.bfloat16)
        low = (once - high.astype(jnp.float32)).astype(jnp.bfloat16)
        twice = jnp.dot(back, high, preferred_element_type=jnp.float32) + jnp.dot(back, low, preferred_element_type=jnp.float32)
        for piece in (0, 1):
            along_z[(first + piece) * rows : (first + piece + 1) * rows, :] = twice[:, piece * LANES : (piece + 1) * LANES]
    slab = width * depth

    def one_x(x):
        total = table[0, pl.ds(x, 1), :] * along_z[0:slab, :]
        for other in range(1, length_x):
            total = total + table[other, pl.ds(x, 1), :] * along_z[other * slab : (other + 1) * slab, :]
        start = pl.multiple_of(x * slab, 16)
        out[pl.ds(start, slab), :] = total.astype(jnp.bfloat16)

    if length_x <= 8:
        for x in range(length_x):
            one_x(x)
    else:
        pl.loop(0, length_x)(one_x)


def mix_y_kernel(dims, planes, offsets, masks, weights, *refs):
    length_x, width, depth = dims
    blocks, (out, fields, mixed, table) = refs[:planes], refs[planes:]
    length_y = planes * width
    cells = length_x * width * depth
    write_gram(table, 1, length_y, (offsets, masks, weights))
    plane = lax.axis_index("pencil")
    chip = lax.axis_index("dp") >> 1
    for away in range(planes):
        wide = blocks[away][...].astype(jnp.float32).reshape(length_x, width, depth, LANES)
        for y in range(width):
            fields[(plane ^ away) * width + y] = wide[:, y]

    def one_x(x, place, y):
        total = table[0, pl.ds(place, 1), :] * fields[0, x]
        for other in range(1, length_y):
            total = total + table[other, pl.ds(place, 1), :] * fields[other, x]
        start = (x * width + y) * depth
        mixed[pl.ds(start if isinstance(start, int) else pl.multiple_of(start, 8), depth), :] = total

    for away in range(planes):
        slab = farthest((chip ^ away) ^ plane, plane, planes)
        for y in range(width):
            place = slab * width + y
            if length_x <= 8:
                for x in range(length_x):
                    one_x(x, place, y)
            else:
                pl.loop(0, length_x)(functools.partial(one_x, place=place, y=y))
        for first in range(0, cells, LANES):
            out[away, :, first : first + LANES] = mixed[first : first + LANES, :].T.astype(jnp.bfloat16)


def gram_kernel(planes, mixed, *refs):
    mine, theirs, out = refs[:planes], refs[planes : 2 * planes], refs[2 * planes]
    total = None
    for away in range(planes):
        both = jnp.concatenate([mine[away][...], theirs[away][...]], axis=1)
        part = jnp.dot(mixed[away], both, preferred_element_type=jnp.float32)
        total = part if total is None else total + part
    core = lax.axis_index("dp") & 1
    out[:, pl.ds(pl.multiple_of(core * LANES, LANES), LANES)] = total[:, :LANES]
    out[:, pl.ds(pl.multiple_of((1 - core) * LANES, LANES), LANES)] = total[:, LANES:]


def call(kernel, out_shape, operands, in_specs, scratch=(), flops=0):
    sizes = [out_shape] + list(operands)
    held = sum(item.size * item.dtype.itemsize for item in sizes)
    spare = sum(4 * int(functools.reduce(lambda a, b: a * b, item.shape)) for item in scratch)
    return pl.pallas_call(
        kernel,
        out_shape=out_shape,
        in_specs=in_specs,
        out_specs=VMEM,
        scratch_shapes=list(scratch),
        compiler_params=pltpu.CompilerParams(vmem_limit_bytes=(6 << 20) + 2 * held + spare),
        cost_estimate=pl.CostEstimate(flops=flops, bytes_accessed=held, transcendentals=0),
    )(*operands)


def shards(jacobian, band_offsets, band_masks, band_weights):
    length_x, width, depth, rows = jacobian.shape
    planes, spread = lax.axis_size("pencil"), lax.axis_size("dp")
    dims = (length_x, width, depth)
    cells = length_x * width * depth
    params = (band_offsets, band_masks, band_weights)
    field = jacobian.reshape(cells, rows)

    route = []
    for source in range(spread):
        for plane in range(planes):
            target_plane = source // CORES
            rank = [farthest(r, target_plane, planes) for r in range(planes)].index(plane)
            target = (target_plane ^ rank) * CORES + source % CORES
            route.append((source * planes + plane, target * planes + target_plane))
    arrived = lax.ppermute(field, ("dp", "pencil"), route)

    mixed_x_z = call(
        functools.partial(mix_x_z_kernel, dims),
        jax.ShapeDtypeStruct((cells, rows), jnp.bfloat16),
        (*params, field),
        [SMEM] * 3 + [VMEM],
        [pltpu.VMEM((cells, LANES), jnp.float32), pltpu.VMEM((length_x, length_x, LANES), jnp.float32)],
    )
    along = [mixed_x_z] + [
        lax.ppermute(mixed_x_z, "pencil", [(i, i ^ away) for i in range(planes)]) for away in range(1, planes)
    ]
    mine = [arrived] + [
        lax.ppermute(arrived, "dp", [(i, i ^ (away * CORES)) for i in range(spread)]) for away in range(1, planes)
    ]
    theirs = [lax.ppermute(block, "dp", [(i, i ^ 1) for i in range(spread)]) for block in mine]
    length_y = planes * width
    mixed = call(
        functools.partial(mix_y_kernel, dims, planes),
        jax.ShapeDtypeStruct((planes, rows, cells), jnp.bfloat16),
        (*params, *along),
        [SMEM] * 3 + [VMEM] * planes,
        [
            pltpu.VMEM((length_y, length_x, depth, LANES), jnp.float32),
            pltpu.VMEM((cells, LANES), jnp.float32),
            pltpu.VMEM((length_y, length_y, LANES), jnp.float32),
        ],
    )
    return call(
        functools.partial(gram_kernel, planes),
        jax.ShapeDtypeStruct((rows, CORES * rows), jnp.float32),
        (mixed, *mine, *theirs),
        [VMEM] * (1 + 2 * planes),
    )


def solution(mesh):
    in_specs = (P(None, "pencil", None, "dp"), P(), P(), P())
    out_specs = P("dp", "pencil")
    return jax.shard_map(shards, mesh=mesh, in_specs=in_specs, out_specs=out_specs, check_vma=False)
```

```python
import functools
import math

import jax
import jax.numpy as jnp
from jax import lax
from jax.experimental import pallas as pl
from jax.experimental.pallas import tpu as pltpu
from jax.sharding import PartitionSpec as P

BANDS = 3
BLOCKS = 4
LANES = 128
CORES = 2
COLUMNS_AT_ONCE = 8
VMEM = pl.BlockSpec(memory_space=pltpu.VMEM)
HBM = pl.BlockSpec(memory_space=pltpu.HBM)


def farthest(rank, plane, planes):
    mirrored = planes - 1 - plane
    if isinstance(plane, int) and isinstance(rank, int):
        alone, reach, outer = abs(plane - mirrored), min(plane, mirrored), rank if plane > mirrored else planes - 1 - rank
        pair = rank - alone
        inner = plane - (reach - pair // 2) if pair % 2 == 0 else plane + (reach - pair // 2)
        return outer if rank < alone else inner
    alone, reach = jnp.abs(plane - mirrored), jnp.minimum(plane, mirrored)
    outer = jnp.where(plane > mirrored, rank, planes - 1 - rank)
    pair = rank - alone
    away = reach - (pair >> 1)
    inner = jnp.where((pair & 1) == 0, plane - away, plane + away)
    return jnp.where(rank < alone, outer, inner)


def smoother(distance, owner, axis, length, offsets, masks, weights):
    matrix = jnp.where(distance == 0, jnp.float32(1.0), jnp.float32(0.0))
    for band in range(BANDS):
        value = masks[axis, band, 0].astype(jnp.float32) * weights[axis, band]
        for block in range(1, BLOCKS):
            here = masks[axis, band, block].astype(jnp.float32) * weights[axis, band]
            value = jnp.where(owner >= block * (length // BLOCKS), here, value)
        matrix = matrix + jnp.where(distance == offsets[axis, band], value, jnp.float32(0.0))
    return matrix.astype(jnp.bfloat16)


def write_columns(table, matrix, length):
    for place in range(length):
        table[place] = jnp.broadcast_to(matrix[:length, place : place + 1], (length, LANES))


def square_distance(length):
    row = lax.broadcasted_iota(jnp.int32, (LANES, LANES), 0)
    col = lax.broadcasted_iota(jnp.int32, (LANES, LANES), 1)
    return row, col, jnp.where((row < length) & (col < length), jnp.abs(row - col), -1)


def smooth_x_z(dims, field, out, blocks_z, table_x, along_z):
    length_x, width, depth = dims
    rows = COLUMNS_AT_ONCE * depth
    pieces = length_x * width // COLUMNS_AT_ONCE
    for first in range(0, pieces, 2):
        held = jnp.concatenate([field[piece * rows : (piece + 1) * rows, :] for piece in (first, first + 1)], axis=1)
        both = jnp.dot(blocks_z[...], held, preferred_element_type=jnp.float32)
        for piece in (0, 1):
            along_z[(first + piece) * rows : (first + piece + 1) * rows, :] = both[:, piece * LANES : (piece + 1) * LANES]
    slab = width * depth

    def one_x(x):
        total = table_x[0, pl.ds(x, 1), :] * along_z[0:slab, :]
        for other in range(1, length_x):
            total = total + table_x[other, pl.ds(x, 1), :] * along_z[other * slab : (other + 1) * slab, :]
        start = x * slab if isinstance(x, int) else pl.multiple_of(x * slab, 16)
        out[pl.ds(start, slab), :] = total.astype(jnp.bfloat16)

    if length_x <= 8:
        for x in range(length_x):
            one_x(x)
    else:
        pl.loop(0, length_x)(one_x)


def first_kernel(dims, length_y, *refs):
    length_x, width, depth = dims
    sources, (out, blocks_z, table_x, table_y) = refs[:4], refs[4:8]
    held, (along_z, arrivals) = refs[8:12], refs[12:]
    copies = [
        pltpu.make_async_copy(source, place, arrivals.at[which])
        for which, (source, place) in enumerate(zip(sources, held))
    ]
    for copy in copies:
        copy.start()
    for copy in copies[:3]:
        copy.wait()
    params, field = held[:3], held[3]
    row, col, distance = square_distance(length_x)
    write_columns(table_x, smoother(distance, row, 0, length_x, *params).astype(jnp.float32), length_x)
    row, col, distance = square_distance(length_y)
    gram = jnp.dot(
        smoother(distance, col, 1, length_y, *params),
        smoother(distance, row, 1, length_y, *params),
        preferred_element_type=jnp.float32,
    )
    write_columns(table_y, gram, length_y)
    rows = COLUMNS_AT_ONCE * depth
    shape = (COLUMNS_AT_ONCE, depth, rows)
    row_z = lax.broadcasted_iota(jnp.int32, shape, 1)
    row_group = lax.broadcasted_iota(jnp.int32, shape, 0)
    lane = lax.broadcasted_iota(jnp.int32, shape, 2)
    lane_group = jnp.zeros(shape, jnp.int32)
    for group in range(1, COLUMNS_AT_ONCE):
        lane_group = lane_group + jnp.where(lane >= group * depth, 1, 0)
    distance = jnp.where(row_group == lane_group, jnp.abs(row_z - (lane - lane_group * depth)), -1)
    matrix = smoother(distance, row_z, 2, depth, *params).astype(jnp.float32)
    blocks_z[...] = matrix.reshape(rows, rows).astype(jnp.bfloat16)
    copies[3].wait()
    smooth_x_z(dims, field, out, blocks_z, table_x, along_z)


def second_kernel(dims, field, blocks_z, table_x, out, along_z):
    smooth_x_z(dims, field, out, blocks_z, table_x, along_z)


def mix_y_kernel(dims, planes, table, *refs):
    length_x, width, depth = dims
    blocks, mine, (out, fields, mixed) = refs[:planes], refs[planes : 2 * planes], refs[2 * planes :]
    length_y = planes * width
    cells = length_x * width * depth
    plane = lax.axis_index("pencil")
    chip = lax.axis_index("dp") >> 1
    slabs = [farthest((chip ^ away) ^ plane, plane, planes) for away in range(planes)]

    def widen(block, slab):
        wide = block[...].astype(jnp.float32).reshape(length_x, width, depth, LANES)
        for y in range(width):
            fields[slab * width + y] = wide[:, y]

    @pl.when(chip == plane)
    def _():
        for away in range(planes):
            widen(mine[away], slabs[away])

    @pl.when(chip != plane)
    def _():
        for away in range(planes):
            widen(blocks[away], plane ^ away)

    def one_x(x, place, y):
        total = table[0, pl.ds(place, 1), :] * fields[0, x]
        for other in range(1, length_y):
            total = total + table[other, pl.ds(place, 1), :] * fields[other, x]
        start = (x * width + y) * depth
        mixed[pl.ds(start if isinstance(start, int) else pl.multiple_of(start, 8), depth), :] = total

    for away in range(planes):
        for y in range(width):
            place = slabs[away] * width + y
            if length_x <= 8:
                for x in range(length_x):
                    one_x(x, place, y)
            else:
                pl.loop(0, length_x)(functools.partial(one_x, place=place, y=y))
        for first in range(0, cells, LANES):
            out[away, :, first : first + LANES] = mixed[first : first + LANES, :].T.astype(jnp.bfloat16)


def gram_kernel(planes, mixed, *refs):
    mine, theirs, out = refs[:planes], refs[planes : 2 * planes], refs[2 * planes]
    total = None
    for away in range(planes):
        both = jnp.concatenate([mine[away][...], theirs[away][...]], axis=1)
        part = jnp.dot(mixed[away], both, preferred_element_type=jnp.float32)
        total = part if total is None else total + part
    core = lax.axis_index("dp") & 1
    out[:, pl.ds(pl.multiple_of(core * LANES, LANES), LANES)] = total[:, :LANES]
    out[:, pl.ds(pl.multiple_of((1 - core) * LANES, LANES), LANES)] = total[:, LANES:]


def call(kernel, out_shape, operands, in_specs, scratch=(), flops=0):
    sizes = jax.tree.leaves(out_shape) + list(operands)
    held = sum(item.size * item.dtype.itemsize for item in sizes)
    spare = sum(4 * math.prod(item.shape) for item in scratch if item.memory_space == pltpu.VMEM)
    return pl.pallas_call(
        kernel,
        out_shape=out_shape,
        in_specs=in_specs,
        out_specs=jax.tree.map(lambda _: VMEM, out_shape),
        scratch_shapes=list(scratch),
        compiler_params=pltpu.CompilerParams(vmem_limit_bytes=(6 << 20) + 2 * held + spare),
        cost_estimate=pl.CostEstimate(flops=flops, bytes_accessed=held, transcendentals=0),
    )(*operands)


def after(item, *others):
    return lax.optimization_barrier((item, *others))[0]


def shards(jacobian, band_offsets, band_masks, band_weights):
    length_x, width, depth, rows = jacobian.shape
    planes, spread = lax.axis_size("pencil"), lax.axis_size("dp")
    dims = (length_x, width, depth)
    cells = length_x * width * depth
    params = (band_offsets, band_masks, band_weights)
    field = jacobian.reshape(cells, rows)
    length_y = planes * width

    route = []
    for source in range(spread):
        for plane in range(planes):
            target_plane = source // CORES
            rank = [farthest(r, target_plane, planes) for r in range(planes)].index(plane)
            target = (target_plane ^ rank) * CORES + source % CORES
            route.append((source * planes + plane, target * planes + target_plane))
    arrived = lax.ppermute(field, ("dp", "pencil"), route)

    block = COLUMNS_AT_ONCE * depth
    smooth, blocks_z, table_x, table_y = call(
        functools.partial(first_kernel, dims, length_y),
        (
            jax.ShapeDtypeStruct((cells, rows), jnp.bfloat16),
            jax.ShapeDtypeStruct((block, block), jnp.bfloat16),
            jax.ShapeDtypeStruct((length_x, length_x, LANES), jnp.float32),
            jax.ShapeDtypeStruct((length_y, length_y, LANES), jnp.float32),
        ),
        tuple(pltpu.with_memory_space_constraint(item, pltpu.HBM) for item in (*params, field)),
        [HBM] * 4,
        [pltpu.SMEM(item.shape, item.dtype) for item in params]
        + [
            pltpu.VMEM((cells, rows), jnp.bfloat16),
            pltpu.VMEM((cells, LANES), jnp.float32),
            pltpu.SemaphoreType.DMA((4,)),
        ],
    )
    along = [smooth] + [None] * (planes - 1)
    for away in range(planes - 1, 0, -1):
        pairs = []
        for d in range(spread):
            for p in range(planes):
                needed = d // CORES != p ^ away
                target = (d, p ^ away) if needed else (p * CORES + d % CORES, p)
                pairs.append((d * planes + p, target[0] * planes + target[1]))
        along[away] = lax.ppermute(smooth, ("dp", "pencil"), pairs)
    mixed_arrived = call(
        functools.partial(second_kernel, dims),
        jax.ShapeDtypeStruct((cells, rows), jnp.bfloat16),
        (arrived, blocks_z, table_x),
        [VMEM] * 3,
        [pltpu.VMEM((cells, LANES), jnp.float32)],
    )
    mine = [mixed_arrived] + [
        lax.ppermute(mixed_arrived, "dp", [(i, i ^ (away * CORES)) for i in range(spread)]) for away in range(1, planes)
    ]
    theirs = []
    for which, item in enumerate(mine):
        item = after(item, *along[1:]) if which > 0 else item
        theirs.append(lax.ppermute(item, "dp", [(i, i ^ 1) for i in range(spread)]))
    mixed = call(
        functools.partial(mix_y_kernel, dims, planes),
        jax.ShapeDtypeStruct((planes, rows, cells), jnp.bfloat16),
        (table_y, *along, *mine),
        [VMEM] * (1 + 2 * planes),
        [
            pltpu.VMEM((length_y, length_x, depth, LANES), jnp.float32),
            pltpu.VMEM((cells, LANES), jnp.float32),
        ],
    )
    return call(
        functools.partial(gram_kernel, planes),
        jax.ShapeDtypeStruct((rows, CORES * rows), jnp.float32),
        (mixed, *mine, *theirs),
        [VMEM] * (1 + 2 * planes),
    )


def solution(mesh):
    in_specs = (P(None, "pencil", None, "dp"), P(), P(), P())
    out_specs = P("dp", "pencil")
    return jax.shard_map(shards, mesh=mesh, in_specs=in_specs, out_specs=out_specs, check_vma=False)
```

```python
import functools
import math

import jax
import jax.numpy as jnp
from jax import lax
from jax.experimental import pallas as pl
from jax.experimental.pallas import tpu as pltpu
from jax.sharding import PartitionSpec as P

BANDS = 3
BLOCKS = 4
LANES = 128
CORES = 2
COLUMNS_AT_ONCE = 8
VMEM = pl.BlockSpec(memory_space=pltpu.VMEM)
HBM = pl.BlockSpec(memory_space=pltpu.HBM)


def farthest(rank, plane, planes):
    mirrored = planes - 1 - plane
    if isinstance(plane, int) and isinstance(rank, int):
        alone, reach, outer = abs(plane - mirrored), min(plane, mirrored), rank if plane > mirrored else planes - 1 - rank
        pair = rank - alone
        inner = plane - (reach - pair // 2) if pair % 2 == 0 else plane + (reach - pair // 2)
        return outer if rank < alone else inner
    alone, reach = jnp.abs(plane - mirrored), jnp.minimum(plane, mirrored)
    outer = jnp.where(plane > mirrored, rank, planes - 1 - rank)
    pair = rank - alone
    away = reach - (pair >> 1)
    inner = jnp.where((pair & 1) == 0, plane - away, plane + away)
    return jnp.where(rank < alone, outer, inner)


def smoother(distance, owner, axis, length, offsets, masks, weights):
    matrix = jnp.where(distance == 0, jnp.float32(1.0), jnp.float32(0.0))
    for band in range(BANDS):
        value = masks[axis, band, 0].astype(jnp.float32) * weights[axis, band]
        for block in range(1, BLOCKS):
            here = masks[axis, band, block].astype(jnp.float32) * weights[axis, band]
            value = jnp.where(owner >= block * (length // BLOCKS), here, value)
        matrix = matrix + jnp.where(distance == offsets[axis, band], value, jnp.float32(0.0))
    return matrix.astype(jnp.bfloat16)


def write_columns(table, matrix, length):
    for place in range(length):
        table[place] = jnp.broadcast_to(matrix[:length, place : place + 1], (length, LANES))


def square_distance(length):
    row = lax.broadcasted_iota(jnp.int32, (LANES, LANES), 0)
    col = lax.broadcasted_iota(jnp.int32, (LANES, LANES), 1)
    return row, col, jnp.where((row < length) & (col < length), jnp.abs(row - col), -1)


def smooth_x_z(dims, field, out, blocks_z, table_x, along_z):
    length_x, width, depth = dims
    rows = COLUMNS_AT_ONCE * depth
    pieces = length_x * width // COLUMNS_AT_ONCE
    for first in range(0, pieces, 2):
        held = jnp.concatenate([field[piece * rows : (piece + 1) * rows, :] for piece in (first, first + 1)], axis=1)
        both = jnp.dot(blocks_z[...], held, preferred_element_type=jnp.float32)
        for piece in (0, 1):
            along_z[(first + piece) * rows : (first + piece + 1) * rows, :] = both[:, piece * LANES : (piece + 1) * LANES]
    slab = width * depth

    def one_x(x):
        total = table_x[0, pl.ds(x, 1), :] * along_z[0:slab, :]
        for other in range(1, length_x):
            total = total + table_x[other, pl.ds(x, 1), :] * along_z[other * slab : (other + 1) * slab, :]
        start = x * slab if isinstance(x, int) else pl.multiple_of(x * slab, 16)
        out[pl.ds(start, slab), :] = total.astype(jnp.bfloat16)

    if length_x <= 8:
        for x in range(length_x):
            one_x(x)
    else:
        pl.loop(0, length_x)(one_x)


def first_kernel(dims, length_y, *refs):
    length_x, width, depth = dims
    sources, (out, blocks_z, table_x, table_y) = refs[:4], refs[4:8]
    held, (along_z, arrivals) = refs[8:12], refs[12:]
    copies = [
        pltpu.make_async_copy(source, place, arrivals.at[which])
        for which, (source, place) in enumerate(zip(sources, held))
    ]
    for copy in copies:
        copy.start()
    for copy in copies[:3]:
        copy.wait()
    params, field = held[:3], held[3]
    row, col, distance = square_distance(length_x)
    write_columns(table_x, smoother(distance, row, 0, length_x, *params).astype(jnp.float32), length_x)
    row, col, distance = square_distance(length_y)
    gram = jnp.dot(
        smoother(distance, col, 1, length_y, *params),
        smoother(distance, row, 1, length_y, *params),
        preferred_element_type=jnp.float32,
    )
    write_columns(table_y, gram, length_y)
    rows = COLUMNS_AT_ONCE * depth
    shape = (COLUMNS_AT_ONCE, depth, rows)
    row_z = lax.broadcasted_iota(jnp.int32, shape, 1)
    row_group = lax.broadcasted_iota(jnp.int32, shape, 0)
    lane = lax.broadcasted_iota(jnp.int32, shape, 2)
    lane_group = jnp.zeros(shape, jnp.int32)
    for group in range(1, COLUMNS_AT_ONCE):
        lane_group = lane_group + jnp.where(lane >= group * depth, 1, 0)
    distance = jnp.where(row_group == lane_group, jnp.abs(row_z - (lane - lane_group * depth)), -1)
    matrix = smoother(distance, row_z, 2, depth, *params).astype(jnp.float32)
    blocks_z[...] = matrix.reshape(rows, rows).astype(jnp.bfloat16)
    copies[3].wait()
    smooth_x_z(dims, field, out, blocks_z, table_x, along_z)


def second_kernel(dims, field, blocks_z, table_x, out, along_z):
    smooth_x_z(dims, field, out, blocks_z, table_x, along_z)


def mix_y_kernel(dims, planes, far_order, near_order, table, *refs):
    length_x, width, depth = dims
    blocks, mine, (out, fields, mixed) = refs[:planes], refs[planes : 2 * planes], refs[2 * planes :]
    length_y = planes * width
    cells = length_x * width * depth
    plane = lax.axis_index("pencil")
    chip = lax.axis_index("dp") >> 1
    slabs = [farthest((chip ^ away) ^ plane, plane, planes) for away in near_order]

    def widen(block, slab):
        wide = block[...].astype(jnp.float32).reshape(length_x, width, depth, LANES)
        for y in range(width):
            fields[slab * width + y] = wide[:, y]

    @pl.when(chip == plane)
    def _():
        for block, slab in zip(mine, slabs):
            widen(block, slab)

    @pl.when(chip != plane)
    def _():
        for block, away in zip(blocks, far_order):
            widen(block, plane ^ away)

    def one_x(x, place, y):
        total = table[0, pl.ds(place, 1), :] * fields[0, x]
        for other in range(1, length_y):
            total = total + table[other, pl.ds(place, 1), :] * fields[other, x]
        start = (x * width + y) * depth
        mixed[pl.ds(start if isinstance(start, int) else pl.multiple_of(start, 8), depth), :] = total

    for away in range(planes):
        for y in range(width):
            place = slabs[away] * width + y
            if length_x <= 8:
                for x in range(length_x):
                    one_x(x, place, y)
            else:
                pl.loop(0, length_x)(functools.partial(one_x, place=place, y=y))
        for first in range(0, cells, LANES):
            out[away, :, first : first + LANES] = mixed[first : first + LANES, :].T.astype(jnp.bfloat16)


def gram_kernel(planes, mixed, *refs):
    mine, theirs, out = refs[:planes], refs[planes : 2 * planes], refs[2 * planes]
    total = None
    for away in range(planes):
        both = jnp.concatenate([mine[away][...], theirs[away][...]], axis=1)
        part = jnp.dot(mixed[away], both, preferred_element_type=jnp.float32)
        total = part if total is None else total + part
    core = lax.axis_index("dp") & 1
    out[:, pl.ds(pl.multiple_of(core * LANES, LANES), LANES)] = total[:, :LANES]
    out[:, pl.ds(pl.multiple_of((1 - core) * LANES, LANES), LANES)] = total[:, LANES:]


def call(kernel, out_shape, operands, in_specs, scratch=(), flops=0):
    sizes = jax.tree.leaves(out_shape) + list(operands)
    held = sum(item.size * item.dtype.itemsize for item in sizes)
    spare = sum(4 * math.prod(item.shape) for item in scratch if item.memory_space == pltpu.VMEM)
    return pl.pallas_call(
        kernel,
        out_shape=out_shape,
        in_specs=in_specs,
        out_specs=jax.tree.map(lambda _: VMEM, out_shape),
        scratch_shapes=list(scratch),
        compiler_params=pltpu.CompilerParams(vmem_limit_bytes=(6 << 20) + 2 * held + spare),
        cost_estimate=pl.CostEstimate(flops=flops, bytes_accessed=held, transcendentals=0),
    )(*operands)


def after(item, *others):
    return lax.optimization_barrier((item, *others))[0]


def shards(jacobian, band_offsets, band_masks, band_weights):
    length_x, width, depth, rows = jacobian.shape
    planes, spread = lax.axis_size("pencil"), lax.axis_size("dp")
    dims = (length_x, width, depth)
    cells = length_x * width * depth
    params = (band_offsets, band_masks, band_weights)
    field = jacobian.reshape(cells, rows)
    length_y = planes * width

    route = []
    for source in range(spread):
        for plane in range(planes):
            target_plane = source // CORES
            rank = [farthest(r, target_plane, planes) for r in range(planes)].index(plane)
            target = (target_plane ^ rank) * CORES + source % CORES
            route.append((source * planes + plane, target * planes + target_plane))
    arrived = lax.ppermute(field, ("dp", "pencil"), route)

    block = COLUMNS_AT_ONCE * depth
    smooth, blocks_z, table_x, table_y = call(
        functools.partial(first_kernel, dims, length_y),
        (
            jax.ShapeDtypeStruct((cells, rows), jnp.bfloat16),
            jax.ShapeDtypeStruct((block, block), jnp.bfloat16),
            jax.ShapeDtypeStruct((length_x, length_x, LANES), jnp.float32),
            jax.ShapeDtypeStruct((length_y, length_y, LANES), jnp.float32),
        ),
        tuple(pltpu.with_memory_space_constraint(item, pltpu.HBM) for item in (*params, field)),
        [HBM] * 4,
        [pltpu.SMEM(item.shape, item.dtype) for item in params]
        + [
            pltpu.VMEM((cells, rows), jnp.bfloat16),
            pltpu.VMEM((cells, LANES), jnp.float32),
            pltpu.SemaphoreType.DMA((4,)),
        ],
    )
    far_order = (0, *range(1, planes, 2), *range(2, planes, 2))
    near_order = (0, *range(planes - 1, 0, -1))
    along = [smooth]
    for away in far_order[1:]:
        pairs = []
        for d in range(spread):
            for p in range(planes):
                needed = d // CORES != p ^ away
                target = (d, p ^ away) if needed else (p * CORES + d % CORES, p)
                pairs.append((d * planes + p, target[0] * planes + target[1]))
        along.append(lax.ppermute(smooth, ("dp", "pencil"), pairs))
    mixed_arrived = call(
        functools.partial(second_kernel, dims),
        jax.ShapeDtypeStruct((cells, rows), jnp.bfloat16),
        (arrived, blocks_z, table_x),
        [VMEM] * 3,
        [pltpu.VMEM((cells, LANES), jnp.float32)],
    )
    mine = [mixed_arrived] + [
        lax.ppermute(mixed_arrived, "dp", [(i, i ^ (away * CORES)) for i in range(spread)]) for away in near_order[1:]
    ]
    theirs = []
    for which, item in enumerate(mine):
        item = after(item, *along[1:]) if which > 0 else item
        theirs.append(lax.ppermute(item, "dp", [(i, i ^ 1) for i in range(spread)]))
    mixed = call(
        functools.partial(mix_y_kernel, dims, planes, far_order, near_order),
        jax.ShapeDtypeStruct((planes, rows, cells), jnp.bfloat16),
        (table_y, *along, *mine),
        [VMEM] * (1 + 2 * planes),
        [
            pltpu.VMEM((length_y, length_x, depth, LANES), jnp.float32),
            pltpu.VMEM((cells, LANES), jnp.float32),
        ],
    )
    return call(
        functools.partial(gram_kernel, planes),
        jax.ShapeDtypeStruct((rows, CORES * rows), jnp.float32),
        (mixed, *mine, *theirs),
        [VMEM] * (1 + 2 * planes),
    )


def solution(mesh):
    in_specs = (P(None, "pencil", None, "dp"), P(), P(), P())
    out_specs = P("dp", "pencil")
    return jax.shard_map(shards, mesh=mesh, in_specs=in_specs, out_specs=out_specs, check_vma=False)
```

```python
import functools
import math

import jax
import jax.numpy as jnp
from jax import lax
from jax.experimental import pallas as pl
from jax.experimental.pallas import tpu as pltpu
from jax.sharding import PartitionSpec as P

BANDS = 3
PLACES = (3, 2, 0, 1)
BLOCKS = 4
LANES = 128
CORES = 2
COLUMNS_AT_ONCE = 8
VMEM = pl.BlockSpec(memory_space=pltpu.VMEM)
HBM = pl.BlockSpec(memory_space=pltpu.HBM)


def farthest(rank, plane, planes):
    mirrored = planes - 1 - plane
    if isinstance(plane, int) and isinstance(rank, int):
        alone, reach, outer = abs(plane - mirrored), min(plane, mirrored), rank if plane > mirrored else planes - 1 - rank
        pair = rank - alone
        inner = plane - (reach - pair // 2) if pair % 2 == 0 else plane + (reach - pair // 2)
        return outer if rank < alone else inner
    alone, reach = jnp.abs(plane - mirrored), jnp.minimum(plane, mirrored)
    outer = jnp.where(plane > mirrored, rank, planes - 1 - rank)
    pair = rank - alone
    away = reach - (pair >> 1)
    inner = jnp.where((pair & 1) == 0, plane - away, plane + away)
    return jnp.where(rank < alone, outer, inner)


def decode(value):
    rank = value
    for which, code in enumerate(PLACES):
        rank = jnp.where(value == code, which, rank)
    return rank


def smoother(distance, owner, axis, length, offsets, masks, weights):
    matrix = jnp.where(distance == 0, jnp.float32(1.0), jnp.float32(0.0))
    for band in range(BANDS):
        value = masks[axis, band, 0].astype(jnp.float32) * weights[axis, band]
        for block in range(1, BLOCKS):
            here = masks[axis, band, block].astype(jnp.float32) * weights[axis, band]
            value = jnp.where(owner >= block * (length // BLOCKS), here, value)
        matrix = matrix + jnp.where(distance == offsets[axis, band], value, jnp.float32(0.0))
    return matrix.astype(jnp.bfloat16)


def write_columns(table, matrix, length):
    for place in range(length):
        table[place] = jnp.broadcast_to(matrix[:length, place : place + 1], (length, LANES))


def square_distance(length):
    row = lax.broadcasted_iota(jnp.int32, (LANES, LANES), 0)
    col = lax.broadcasted_iota(jnp.int32, (LANES, LANES), 1)
    return row, col, jnp.where((row < length) & (col < length), jnp.abs(row - col), -1)


def smooth_x_z(dims, field, out, blocks_z, table_x, along_z):
    length_x, width, depth = dims
    rows = COLUMNS_AT_ONCE * depth
    pieces = length_x * width // COLUMNS_AT_ONCE
    for first in range(0, pieces, 2):
        held = jnp.concatenate([field[piece * rows : (piece + 1) * rows, :] for piece in (first, first + 1)], axis=1)
        both = jnp.dot(blocks_z[...], held, preferred_element_type=jnp.float32)
        for piece in (0, 1):
            along_z[(first + piece) * rows : (first + piece + 1) * rows, :] = both[:, piece * LANES : (piece + 1) * LANES]
    slab = width * depth

    def one_x(x):
        total = table_x[0, pl.ds(x, 1), :] * along_z[0:slab, :]
        for other in range(1, length_x):
            total = total + table_x[other, pl.ds(x, 1), :] * along_z[other * slab : (other + 1) * slab, :]
        start = x * slab if isinstance(x, int) else pl.multiple_of(x * slab, 16)
        out[pl.ds(start, slab), :] = total.astype(jnp.bfloat16)

    if length_x <= 8:
        for x in range(length_x):
            one_x(x)
    else:
        pl.loop(0, length_x)(one_x)


def first_kernel(dims, length_y, *refs):
    length_x, width, depth = dims
    sources, (out, blocks_z, table_x, table_y) = refs[:4], refs[4:8]
    held, (along_z, arrivals) = refs[8:12], refs[12:]
    copies = [
        pltpu.make_async_copy(source, place, arrivals.at[which])
        for which, (source, place) in enumerate(zip(sources, held))
    ]
    for copy in copies:
        copy.start()
    for copy in copies[:3]:
        copy.wait()
    params, field = held[:3], held[3]
    row, col, distance = square_distance(length_x)
    write_columns(table_x, smoother(distance, row, 0, length_x, *params).astype(jnp.float32), length_x)
    row, col, distance = square_distance(length_y)
    gram = jnp.dot(
        smoother(distance, col, 1, length_y, *params),
        smoother(distance, row, 1, length_y, *params),
        preferred_element_type=jnp.float32,
    )
    write_columns(table_y, gram, length_y)
    rows = COLUMNS_AT_ONCE * depth
    shape = (COLUMNS_AT_ONCE, depth, rows)
    row_z = lax.broadcasted_iota(jnp.int32, shape, 1)
    row_group = lax.broadcasted_iota(jnp.int32, shape, 0)
    lane = lax.broadcasted_iota(jnp.int32, shape, 2)
    lane_group = jnp.zeros(shape, jnp.int32)
    for group in range(1, COLUMNS_AT_ONCE):
        lane_group = lane_group + jnp.where(lane >= group * depth, 1, 0)
    distance = jnp.where(row_group == lane_group, jnp.abs(row_z - (lane - lane_group * depth)), -1)
    matrix = smoother(distance, row_z, 2, depth, *params).astype(jnp.float32)
    blocks_z[...] = matrix.reshape(rows, rows).astype(jnp.bfloat16)
    copies[3].wait()
    smooth_x_z(dims, field, out, blocks_z, table_x, along_z)


def second_kernel(dims, field, blocks_z, table_x, out, along_z):
    smooth_x_z(dims, field, out, blocks_z, table_x, along_z)


def mix_y_kernel(dims, planes, far_order, near_order, table, *refs):
    length_x, width, depth = dims
    blocks, mine, (out, fields, mixed) = refs[:planes], refs[planes : 2 * planes], refs[2 * planes :]
    length_y = planes * width
    cells = length_x * width * depth
    plane = lax.axis_index("pencil")
    chip = lax.axis_index("dp") >> 1
    slabs = [farthest(decode((chip ^ away) ^ plane), plane, planes) for away in near_order]

    def widen(block, slab):
        wide = block[...].astype(jnp.float32).reshape(length_x, width, depth, LANES)
        for y in range(width):
            fields[slab * width + y] = wide[:, y]

    @pl.when(chip == plane)
    def _():
        for block, slab in zip(mine, slabs):
            widen(block, slab)

    @pl.when(chip != plane)
    def _():
        for block, away in zip(blocks, far_order):
            widen(block, plane ^ away)

    def one_x(x, place, y):
        total = table[0, pl.ds(place, 1), :] * fields[0, x]
        for other in range(1, length_y):
            total = total + table[other, pl.ds(place, 1), :] * fields[other, x]
        start = (x * width + y) * depth
        mixed[pl.ds(start if isinstance(start, int) else pl.multiple_of(start, 8), depth), :] = total

    for away in range(planes):
        for y in range(width):
            place = slabs[away] * width + y
            if length_x <= 8:
                for x in range(length_x):
                    one_x(x, place, y)
            else:
                pl.loop(0, length_x)(functools.partial(one_x, place=place, y=y))
        for first in range(0, cells, LANES):
            out[away, :, first : first + LANES] = mixed[first : first + LANES, :].T.astype(jnp.bfloat16)


def gram_kernel(planes, mixed, *refs):
    mine, theirs, out = refs[:planes], refs[planes : 2 * planes], refs[2 * planes]
    total = None
    for away in range(planes):
        both = jnp.concatenate([mine[away][...], theirs[away][...]], axis=1)
        part = jnp.dot(mixed[away], both, preferred_element_type=jnp.float32)
        total = part if total is None else total + part
    core = lax.axis_index("dp") & 1
    out[:, pl.ds(pl.multiple_of(core * LANES, LANES), LANES)] = total[:, :LANES]
    out[:, pl.ds(pl.multiple_of((1 - core) * LANES, LANES), LANES)] = total[:, LANES:]


def call(kernel, out_shape, operands, in_specs, scratch=(), flops=0):
    sizes = jax.tree.leaves(out_shape) + list(operands)
    held = sum(item.size * item.dtype.itemsize for item in sizes)
    spare = sum(4 * math.prod(item.shape) for item in scratch if item.memory_space == pltpu.VMEM)
    return pl.pallas_call(
        kernel,
        out_shape=out_shape,
        in_specs=in_specs,
        out_specs=jax.tree.map(lambda _: VMEM, out_shape),
        scratch_shapes=list(scratch),
        compiler_params=pltpu.CompilerParams(vmem_limit_bytes=(6 << 20) + 2 * held + spare),
        cost_estimate=pl.CostEstimate(flops=flops, bytes_accessed=held, transcendentals=0),
    )(*operands)


def after(item, *others):
    return lax.optimization_barrier((item, *others))[0]


def shards(jacobian, band_offsets, band_masks, band_weights):
    length_x, width, depth, rows = jacobian.shape
    planes, spread = lax.axis_size("pencil"), lax.axis_size("dp")
    dims = (length_x, width, depth)
    cells = length_x * width * depth
    params = (band_offsets, band_masks, band_weights)
    field = jacobian.reshape(cells, rows)
    length_y = planes * width

    route = []
    for source in range(spread):
        for plane in range(planes):
            target_plane = source // CORES
            rank = [farthest(r, target_plane, planes) for r in range(planes)].index(plane)
            target = (target_plane ^ (PLACES[rank] if rank < len(PLACES) else rank)) * CORES + source % CORES
            route.append((source * planes + plane, target * planes + target_plane))
    arrived = lax.ppermute(field, ("dp", "pencil"), route)

    block = COLUMNS_AT_ONCE * depth
    smooth, blocks_z, table_x, table_y = call(
        functools.partial(first_kernel, dims, length_y),
        (
            jax.ShapeDtypeStruct((cells, rows), jnp.bfloat16),
            jax.ShapeDtypeStruct((block, block), jnp.bfloat16),
            jax.ShapeDtypeStruct((length_x, length_x, LANES), jnp.float32),
            jax.ShapeDtypeStruct((length_y, length_y, LANES), jnp.float32),
        ),
        tuple(pltpu.with_memory_space_constraint(item, pltpu.HBM) for item in (*params, field)),
        [HBM] * 4,
        [pltpu.SMEM(item.shape, item.dtype) for item in params]
        + [
            pltpu.VMEM((cells, rows), jnp.bfloat16),
            pltpu.VMEM((cells, LANES), jnp.float32),
            pltpu.SemaphoreType.DMA((4,)),
        ],
    )
    far_order = (0, *range(1, planes, 2), *range(2, planes, 2))
    near_order = far_order
    along = [smooth]
    for away in far_order[1:]:
        pairs = []
        for d in range(spread):
            for p in range(planes):
                needed = d // CORES != p ^ away
                target = (d, p ^ away) if needed else (p * CORES + d % CORES, p)
                pairs.append((d * planes + p, target[0] * planes + target[1]))
        along.append(lax.ppermute(smooth, ("dp", "pencil"), pairs))
    mixed_arrived = call(
        functools.partial(second_kernel, dims),
        jax.ShapeDtypeStruct((cells, rows), jnp.bfloat16),
        (arrived, blocks_z, table_x),
        [VMEM] * 3,
        [pltpu.VMEM((cells, LANES), jnp.float32)],
    )
    mine = [mixed_arrived] + [
        lax.ppermute(mixed_arrived, "dp", [(i, i ^ (away * CORES)) for i in range(spread)]) for away in near_order[1:]
    ]
    theirs = []
    for which, item in enumerate(mine):
        item = after(item, *along[1:]) if which > 0 else item
        theirs.append(lax.ppermute(item, "dp", [(i, i ^ 1) for i in range(spread)]))
    mixed = call(
        functools.partial(mix_y_kernel, dims, planes, far_order, near_order),
        jax.ShapeDtypeStruct((planes, rows, cells), jnp.bfloat16),
        (table_y, *along, *mine),
        [VMEM] * (1 + 2 * planes),
        [
            pltpu.VMEM((length_y, length_x, depth, LANES), jnp.float32),
            pltpu.VMEM((cells, LANES), jnp.float32),
        ],
    )
    return call(
        functools.partial(gram_kernel, planes),
        jax.ShapeDtypeStruct((rows, CORES * rows), jnp.float32),
        (mixed, *mine, *theirs),
        [VMEM] * (1 + 2 * planes),
    )


def solution(mesh):
    in_specs = (P(None, "pencil", None, "dp"), P(), P(), P())
    out_specs = P("dp", "pencil")
    return jax.shard_map(shards, mesh=mesh, in_specs=in_specs, out_specs=out_specs, check_vma=False)
```

```python
import functools
import math

import jax
import jax.numpy as jnp
from jax import lax
from jax.experimental import pallas as pl
from jax.experimental.pallas import tpu as pltpu
from jax.sharding import PartitionSpec as P

BANDS = 3
PLACES = (3, 2, 0, 1)
BLOCKS = 4
LANES = 128
CORES = 2
COLUMNS_AT_ONCE = 8
VMEM = pl.BlockSpec(memory_space=pltpu.VMEM)
HBM = pl.BlockSpec(memory_space=pltpu.HBM)


def farthest(rank, plane, planes):
    mirrored = planes - 1 - plane
    if isinstance(plane, int) and isinstance(rank, int):
        alone, reach, outer = abs(plane - mirrored), min(plane, mirrored), rank if plane > mirrored else planes - 1 - rank
        pair = rank - alone
        inner = plane - (reach - pair // 2) if pair % 2 == 0 else plane + (reach - pair // 2)
        return outer if rank < alone else inner
    alone, reach = jnp.abs(plane - mirrored), jnp.minimum(plane, mirrored)
    outer = jnp.where(plane > mirrored, rank, planes - 1 - rank)
    pair = rank - alone
    away = reach - (pair >> 1)
    inner = jnp.where((pair & 1) == 0, plane - away, plane + away)
    return jnp.where(rank < alone, outer, inner)


def decode(value):
    rank = value
    for which, code in enumerate(PLACES):
        rank = jnp.where(value == code, which, rank)
    return rank


def smoother(distance, owner, axis, length, offsets, masks, weights):
    matrix = jnp.where(distance == 0, jnp.float32(1.0), jnp.float32(0.0))
    for band in range(BANDS):
        value = masks[axis, band, 0].astype(jnp.float32) * weights[axis, band]
        for block in range(1, BLOCKS):
            here = masks[axis, band, block].astype(jnp.float32) * weights[axis, band]
            value = jnp.where(owner >= block * (length // BLOCKS), here, value)
        matrix = matrix + jnp.where(distance == offsets[axis, band], value, jnp.float32(0.0))
    return matrix.astype(jnp.bfloat16)


def write_columns(table, matrix, length):
    for place in range(length):
        table[place] = jnp.broadcast_to(matrix[:length, place : place + 1], (length, LANES))


def square_distance(length):
    row = lax.broadcasted_iota(jnp.int32, (LANES, LANES), 0)
    col = lax.broadcasted_iota(jnp.int32, (LANES, LANES), 1)
    return row, col, jnp.where((row < length) & (col < length), jnp.abs(row - col), -1)


def smooth_x_z(dims, field, out, blocks_z, table_x, along_z):
    length_x, width, depth = dims
    rows = COLUMNS_AT_ONCE * depth
    pieces = length_x * width // COLUMNS_AT_ONCE
    for first in range(0, pieces, 2):
        held = jnp.concatenate([field[piece * rows : (piece + 1) * rows, :] for piece in (first, first + 1)], axis=1)
        both = jnp.dot(blocks_z[...], held, preferred_element_type=jnp.float32)
        for piece in (0, 1):
            along_z[(first + piece) * rows : (first + piece + 1) * rows, :] = both[:, piece * LANES : (piece + 1) * LANES]
    slab = width * depth

    def one_x(x):
        total = table_x[0, pl.ds(x, 1), :] * along_z[0:slab, :]
        for other in range(1, length_x):
            total = total + table_x[other, pl.ds(x, 1), :] * along_z[other * slab : (other + 1) * slab, :]
        start = x * slab if isinstance(x, int) else pl.multiple_of(x * slab, 16)
        out[pl.ds(start, slab), :] = total.astype(jnp.bfloat16)

    if length_x <= 8:
        for x in range(length_x):
            one_x(x)
    else:
        pl.loop(0, length_x)(one_x)


def first_kernel(dims, length_y, *refs):
    length_x, width, depth = dims
    sources, (out, blocks_z, table_x, table_y) = refs[:4], refs[4:8]
    held, (along_z, arrivals) = refs[8:12], refs[12:]
    copies = [
        pltpu.make_async_copy(source, place, arrivals.at[which])
        for which, (source, place) in enumerate(zip(sources, held))
    ]
    for copy in copies:
        copy.start()
    for copy in copies[:3]:
        copy.wait()
    params, field = held[:3], held[3]
    row, col, distance = square_distance(length_x)
    write_columns(table_x, smoother(distance, row, 0, length_x, *params).astype(jnp.float32), length_x)
    row, col, distance = square_distance(length_y)
    gram = jnp.dot(
        smoother(distance, col, 1, length_y, *params),
        smoother(distance, row, 1, length_y, *params),
        preferred_element_type=jnp.float32,
    )
    write_columns(table_y, gram, length_y)
    rows = COLUMNS_AT_ONCE * depth
    shape = (COLUMNS_AT_ONCE, depth, rows)
    row_z = lax.broadcasted_iota(jnp.int32, shape, 1)
    row_group = lax.broadcasted_iota(jnp.int32, shape, 0)
    lane = lax.broadcasted_iota(jnp.int32, shape, 2)
    lane_group = jnp.zeros(shape, jnp.int32)
    for group in range(1, COLUMNS_AT_ONCE):
        lane_group = lane_group + jnp.where(lane >= group * depth, 1, 0)
    distance = jnp.where(row_group == lane_group, jnp.abs(row_z - (lane - lane_group * depth)), -1)
    matrix = smoother(distance, row_z, 2, depth, *params).astype(jnp.float32)
    blocks_z[...] = matrix.reshape(rows, rows).astype(jnp.bfloat16)
    copies[3].wait()
    smooth_x_z(dims, field, out, blocks_z, table_x, along_z)


def second_kernel(dims, field, blocks_z, table_x, out, along_z):
    smooth_x_z(dims, field, out, blocks_z, table_x, along_z)


def mix_y_kernel(dims, planes, far_order, near_order, table, *refs):
    length_x, width, depth = dims
    blocks, mine, (out, fields, mixed) = refs[:planes], refs[planes : 2 * planes], refs[2 * planes :]
    length_y = planes * width
    cells = length_x * width * depth
    plane = lax.axis_index("pencil")
    chip = lax.axis_index("dp") >> 1
    slabs = [farthest(decode((chip ^ away) ^ plane), plane, planes) for away in near_order]

    def widen(block, slab):
        wide = block[...].astype(jnp.float32).reshape(length_x, width, depth, LANES)
        for y in range(width):
            fields[slab * width + y] = wide[:, y]

    @pl.when(chip == plane)
    def _():
        for block, slab in zip(mine, slabs):
            widen(block, slab)

    @pl.when(chip != plane)
    def _():
        for block, away in zip(blocks, far_order):
            widen(block, plane ^ away)

    def one_x(x, place, y):
        total = table[0, pl.ds(place, 1), :] * fields[0, x]
        for other in range(1, length_y):
            total = total + table[other, pl.ds(place, 1), :] * fields[other, x]
        start = (x * width + y) * depth
        mixed[pl.ds(start if isinstance(start, int) else pl.multiple_of(start, 8), depth), :] = total

    for away in range(planes):
        for y in range(width):
            place = slabs[away] * width + y
            if length_x <= 8:
                for x in range(length_x):
                    one_x(x, place, y)
            else:
                pl.loop(0, length_x)(functools.partial(one_x, place=place, y=y))
        for first in range(0, cells, LANES):
            out[away, :, first : first + LANES] = mixed[first : first + LANES, :].T.astype(jnp.bfloat16)


def gram_kernel(planes, mixed, *refs):
    mine, theirs, (out, halves, arrivals) = refs[:planes], refs[planes : 2 * planes], refs[2 * planes :]
    core = lax.axis_index("dp") & 1
    copies = []
    for half, (blocks, place) in enumerate(((mine, core), (theirs, 1 - core))):
        total = None
        for away in range(planes):
            part = jnp.dot(mixed[away], blocks[away][...], preferred_element_type=jnp.float32)
            total = part if total is None else total + part
        halves[half] = total
        columns = pl.ds(pl.multiple_of(place * LANES, LANES), LANES)
        copies.append(pltpu.make_async_copy(halves.at[half], out.at[:, columns], arrivals.at[half]))
        copies[half].start()
    for copy in copies:
        copy.wait()


def call(kernel, out_shape, operands, in_specs, scratch=(), flops=0, out_spec=VMEM):
    sizes = jax.tree.leaves(out_shape) + list(operands)
    held = sum(item.size * item.dtype.itemsize for item in sizes)
    spare = sum(4 * math.prod(item.shape) for item in scratch if item.memory_space == pltpu.VMEM)
    return pl.pallas_call(
        kernel,
        out_shape=out_shape,
        in_specs=in_specs,
        out_specs=jax.tree.map(lambda _: out_spec, out_shape),
        scratch_shapes=list(scratch),
        compiler_params=pltpu.CompilerParams(vmem_limit_bytes=(6 << 20) + 2 * held + spare),
        cost_estimate=pl.CostEstimate(flops=flops, bytes_accessed=held, transcendentals=0),
    )(*operands)


def after(item, *others):
    return lax.optimization_barrier((item, *others))[0]


def shards(jacobian, band_offsets, band_masks, band_weights):
    length_x, width, depth, rows = jacobian.shape
    planes, spread = lax.axis_size("pencil"), lax.axis_size("dp")
    dims = (length_x, width, depth)
    cells = length_x * width * depth
    params = (band_offsets, band_masks, band_weights)
    field = jacobian.reshape(cells, rows)
    length_y = planes * width

    route = []
    for source in range(spread):
        for plane in range(planes):
            target_plane = source // CORES
            rank = [farthest(r, target_plane, planes) for r in range(planes)].index(plane)
            target = (target_plane ^ (PLACES[rank] if rank < len(PLACES) else rank)) * CORES + source % CORES
            route.append((source * planes + plane, target * planes + target_plane))
    arrived = lax.ppermute(field, ("dp", "pencil"), route)

    block = COLUMNS_AT_ONCE * depth
    smooth, blocks_z, table_x, table_y = call(
        functools.partial(first_kernel, dims, length_y),
        (
            jax.ShapeDtypeStruct((cells, rows), jnp.bfloat16),
            jax.ShapeDtypeStruct((block, block), jnp.bfloat16),
            jax.ShapeDtypeStruct((length_x, length_x, LANES), jnp.float32),
            jax.ShapeDtypeStruct((length_y, length_y, LANES), jnp.float32),
        ),
        tuple(pltpu.with_memory_space_constraint(item, pltpu.HBM) for item in (*params, field)),
        [HBM] * 4,
        [pltpu.SMEM(item.shape, item.dtype) for item in params]
        + [
            pltpu.VMEM((cells, rows), jnp.bfloat16),
            pltpu.VMEM((cells, LANES), jnp.float32),
            pltpu.SemaphoreType.DMA((4,)),
        ],
    )
    far_order = (0, *range(1, planes, 2), *range(2, planes, 2))
    near_order = far_order
    along = [smooth]
    for away in far_order[1:]:
        pairs = []
        for d in range(spread):
            for p in range(planes):
                needed = d // CORES != p ^ away
                target = (d, p ^ away) if needed else (p * CORES + d % CORES, p)
                pairs.append((d * planes + p, target[0] * planes + target[1]))
        along.append(lax.ppermute(smooth, ("dp", "pencil"), pairs))
    mixed_arrived = call(
        functools.partial(second_kernel, dims),
        jax.ShapeDtypeStruct((cells, rows), jnp.bfloat16),
        (arrived, blocks_z, table_x),
        [VMEM] * 3,
        [pltpu.VMEM((cells, LANES), jnp.float32)],
    )
    mine = [mixed_arrived] + [
        lax.ppermute(mixed_arrived, "dp", [(i, i ^ (away * CORES)) for i in range(spread)]) for away in near_order[1:]
    ]
    theirs = []
    for which, item in enumerate(mine):
        item = after(item, *along[1:]) if which > 0 else item
        theirs.append(lax.ppermute(item, "dp", [(i, i ^ 1) for i in range(spread)]))
    mixed = call(
        functools.partial(mix_y_kernel, dims, planes, far_order, near_order),
        jax.ShapeDtypeStruct((planes, rows, cells), jnp.bfloat16),
        (table_y, *along, *mine),
        [VMEM] * (1 + 2 * planes),
        [
            pltpu.VMEM((length_y, length_x, depth, LANES), jnp.float32),
            pltpu.VMEM((cells, LANES), jnp.float32),
        ],
    )
    return call(
        functools.partial(gram_kernel, planes),
        jax.ShapeDtypeStruct((rows, CORES * rows), jnp.float32),
        (mixed, *mine, *theirs),
        [VMEM] * (1 + 2 * planes),
        [pltpu.VMEM((CORES, rows, LANES), jnp.float32), pltpu.SemaphoreType.DMA((CORES,))],
        out_spec=pl.BlockSpec(memory_space=pl.ANY),
    )


def solution(mesh):
    in_specs = (P(None, "pencil", None, "dp"), P(), P(), P())
    out_specs = P("dp", "pencil")
    return jax.shard_map(shards, mesh=mesh, in_specs=in_specs, out_specs=out_specs, check_vma=False)
```
